32 devices in a mesh: ctx: 4 (over y, x), tp: 2 (over core), dp: 4 (over z).
Axes of the slice: x: 2, y: 2, z: 4, core: 2. Of those that a mesh axis runs over, the one named last changes fastest.
Arguments:
- nucleotides: int32 [8192], P(('dp', 'ctx')), parts along dimension 0, may hold values from 0 to 3
- complement: int32 [4], replicated, may hold values from 0 to 3, each once
- embedding: float32 [4, 1024], replicated, may hold values from -6 to 6
- w_gate: float32 [1024, 2048], P(None, 'tp'), may hold values from -0.1875 to 0.1875
- w_value: float32 [1024, 2048], P(None, 'tp'), may hold values from -0.1875 to 0.1875
- w_state: float32 [1024, 256], replicated, may hold values from -0.1875 to 0.1875
- w_step: float32 [1024, 32], P(None, 'tp'), may hold values from -0.1875 to 0.1875
- step_bias: float32 [32], P('tp'), may hold values from -5.5 to -4.5
- decay_rate: float32 [32], P('tp'), may hold values from 0 to 3
- conv_value: float32 [4, 2048], P(None, 'tp'), may hold values from -3 to 3
- conv_state: float32 [4, 256], replicated, may hold values from -3 to 3
- skip_gain: float32 [32], P('tp'), may hold values from 0.5 to 2
- norm_weight: float32 [2048], P('tp'), may hold values from 0.1 to 1.9
- w_out: float32 [2048, 1024], P('tp'), may hold values from -0.125 to 0.125
Outputs:
- mixed: float32 [8192, 1024], P(('dp', 'ctx', 'tp')), parts along dimension 0
The draws below stay inside these ranges and needn't reach their ends.
There are 4 independent parts, one for each index of `dp`. The reference program is written for one: setup_inputs(seed, part) draws one part's arguments, and reference() takes and returns one part's arrays. A program takes and returns all parts, laid end to end along the dimension named above; an argument that names none is the same for every part. Nothing has to cross between parts.
Inputs may be any that keep to these rules, and one draw needn't show every extreme that they name: `complement`: a permutation of the 4 nucleotide ids.
All inputs are finite; a program needn't handle non-finite values.
Results may differ from the reference program's by a relative error of at most 0.00023.
Values sent between devices are 32-bit elements; how exact they have to be, the bound alone decides.
A program may use at most 128 MiB of HBM per device.

```python
import jax
import jax.numpy as jnp
from jax import lax

D = 1024
HEADS = 32
HEAD_DIM = 64
INNER = 2048
STATE = 128
VOCAB = 4
CONV = 4
BLK = 256
TOKENS = 2048


def draw_decay_rate(key, part):
    lowest = 20.0 / TOKENS
    uniform_draw = jax.random.uniform(key, (HEADS,), jnp.float32, 0.0, 1.0)
    result = lowest * jnp.exp(uniform_draw * jnp.log(3.0 / lowest))
    return result


def set_ends(values, key, smallest, top_value):
    longest = values.shape.index(max(values.shape))
    spots = []
    for shift in (0, 1):
        where = [jax.random.randint(jax.random.fold_in(key, axis), (), 0, length) for axis, length in enumerate(values.shape)]
        where[longest] = (where[longest] + shift) % values.shape[longest]
        spots.append(tuple(where))
    return values.at[spots[0]].set(smallest).at[spots[1]].set(top_value)


def shard_levels(key, extent, shards, smallest, top_value):
    factor_of = 1.0
    for axis_at, blocks in shards:
        steps = jax.random.uniform(jax.random.fold_in(jax.random.fold_in(key, 6), axis_at), (blocks,), jnp.float32, smallest / len(shards), top_value / len(shards))
        factor_of = factor_of * jnp.repeat(jnp.exp(steps), extent[axis_at] // blocks).reshape((-1,) + (1,) * (len(extent) - 1 - axis_at))
    return factor_of


def noise(stream_key, dims, width, reach, shards=(), kind=jnp.bfloat16):
    drawn = jax.random.normal(stream_key, dims, jnp.float32) * width
    if len(shards) > 0:
        drawn = shard_levels(stream_key, dims, shards, -0.22, 0.18) * drawn
    return jnp.clip(drawn, min=-reach, max=reach).astype(kind)


def setup_inputs(seed: int = 0, part: int = 0) -> dict:
    streams_of = jax.random.split(jax.random.key(seed), 15)
    own_keys = jax.random.split(jax.random.fold_in(streams_of[14], part), 15)
    return {
        "nucleotides": set_ends(jax.random.randint(own_keys[0], (TOKENS,), 0, VOCAB), jax.random.fold_in(own_keys[0], 1), 0, VOCAB - 1).astype(jnp.int32),
        "complement": jax.random.permutation(streams_of[1], VOCAB).astype(jnp.int32),
        "embedding": noise(streams_of[2], (VOCAB, D), 1.0, 6.0, (), jnp.float32),
        "w_gate": noise(streams_of[3], (D, INNER), D ** -0.5, 0.1875, ((1, 2),), jnp.float32),
        "w_value": noise(streams_of[4], (D, INNER), D ** -0.5, 0.1875, ((1, 2),), jnp.float32),
        "w_state": noise(streams_of[5], (D, 2 * STATE), D ** -0.5, 0.1875, (), jnp.float32),
        "w_step": noise(streams_of[6], (D, HEADS), D ** -0.5, 0.1875, ((1, 2),), jnp.float32),
        "step_bias": jnp.clip(-5.5 + 1.0 * jax.random.uniform(streams_of[7], (HEADS,), jnp.float32) ** shard_levels(streams_of[7], (HEADS,), ((0, 2),), -0.2, 0.2), -5.5, -4.5),
        "decay_rate": draw_decay_rate(jax.random.fold_in(streams_of[14], 71), part),
        "conv_value": noise(streams_of[9], (CONV, INNER), CONV ** -0.5, 3.0, ((1, 2),), jnp.float32),
        "conv_state": noise(streams_of[10], (CONV, 2 * STATE), CONV ** -0.5, 3.0, (), jnp.float32),
        "skip_gain": jnp.clip(0.5 + 1.5 * jax.random.uniform(streams_of[11], (HEADS,), jnp.float32) ** shard_levels(streams_of[11], (HEADS,), ((0, 2),), -0.2, 0.2), 0.5, 2.0),
        "norm_weight": jnp.clip(1.0 + 0.18 * jax.random.normal(streams_of[12], (INNER,), jnp.float32), 0.1, 1.9),
        "w_out": noise(streams_of[13], (INNER, D), INNER ** -0.5, 0.125, ((0, 2),), jnp.float32),
    }


HIGHEST = lax.Precision.HIGHEST
EPSILON = 1e-05

def causal_conv(padded, kernel):
    length = padded.shape[0] - kernel.shape[0] + 1
    output = jnp.zeros((length, padded.shape[1]), jnp.float32)
    for offset in range(kernel.shape[0]):
        output = output + kernel[offset][None, :] * padded[offset:offset + length]
    return output

def full_scan(values, b_in, c_out, log_step, step_size):
    length = values.shape[0]
    block_count = length // BLK
    block_data = (values.reshape(block_count, BLK, HEADS, HEAD_DIM), b_in.reshape(block_count, BLK, STATE), c_out.reshape(block_count, BLK, STATE), log_step.reshape(block_count, BLK, HEADS), step_size.reshape(block_count, BLK, HEADS))
    causal_mask = jnp.arange(BLK)[:, None] >= jnp.arange(BLK)[None, :]

    def advance(memory, block_items):
        block_values, block_b, block_c, block_log, block_step = block_items
        running = jnp.cumsum(block_log, axis=0)
        spread = jnp.where(causal_mask[:, :, None], running[:, None, :] - running[None, :, :], 0.0)
        weights = jnp.where(causal_mask[:, :, None], jnp.exp(spread), 0.0)
        intersection = jnp.dot(block_c, block_b.T, precision=HIGHEST)
        mixing = intersection[:, :, None] * weights * block_step[None, :, :]
        inside = jnp.einsum('ijh,jhp->ihp', mixing, block_values, precision=HIGHEST)
        carried = jnp.einsum('in,hpn->ihp', block_c, memory, precision=HIGHEST) * jnp.exp(running)[:, :, None]
        weighting = jnp.exp(running[-1][None, :] - running) * block_step
        memory = memory * jnp.exp(running[-1])[:, None, None] + jnp.einsum('jh,jhp,jn->hpn', weighting, block_values, block_b, precision=HIGHEST)
        return (memory, inside + carried)
    initial = jnp.zeros((HEADS, HEAD_DIM, STATE), jnp.float32)
    memory, outputs = lax.scan(advance, initial, block_data)
    return outputs.reshape(length, HEADS, HEAD_DIM)

def strand(sequence, embedding, w_gate, w_value, w_state, w_step, step_bias, decay_rate, conv_value, conv_state, skip_gain, norm_weight):
    table = jnp.concatenate([w_gate, w_value, w_state, w_step], axis=1)
    projected = jnp.dot(embedding, table, precision=HIGHEST)
    rows_in = projected[sequence]
    gate = rows_in[:, :INNER]
    value_raw = rows_in[:, INNER:2 * INNER]
    state_raw = rows_in[:, 2 * INNER:2 * INNER + 2 * STATE]
    step_size = jax.nn.softplus(rows_in[:, 2 * INNER + 2 * STATE:] + step_bias[None, :])
    value_pad = jnp.zeros((CONV - 1, INNER), jnp.float32)
    state_pad = jnp.zeros((CONV - 1, 2 * STATE), jnp.float32)
    values = jax.nn.silu(causal_conv(jnp.concatenate([value_pad, value_raw], axis=0), conv_value))
    maps = jax.nn.silu(causal_conv(jnp.concatenate([state_pad, state_raw], axis=0), conv_state))
    b_in = maps[:, :STATE]
    c_out = maps[:, STATE:]
    head_values = values.reshape(-1, HEADS, HEAD_DIM)
    outputs = full_scan(head_values, b_in, c_out, -decay_rate[None, :] * step_size, step_size)
    outputs = outputs + skip_gain[None, :, None] * head_values
    gated = outputs.reshape(-1, INNER) * jax.nn.silu(gate)
    scale = lax.rsqrt(lax.optimization_barrier(jnp.mean(gated * gated, axis=1, keepdims=True)) + EPSILON)
    return gated * scale * norm_weight[None, :]

def reference(nucleotides, complement, embedding, w_gate, w_value, w_state, w_step, step_bias, decay_rate, conv_value, conv_state, skip_gain, norm_weight, w_out):
    forward_normed = strand(nucleotides, embedding, w_gate, w_value, w_state, w_step, step_bias, decay_rate, conv_value, conv_state, skip_gain, norm_weight)
    reverse_ids = complement[nucleotides][::-1]
    reverse_normed = strand(reverse_ids, embedding, w_gate, w_value, w_state, w_step, step_bias, decay_rate, conv_value, conv_state, skip_gain, norm_weight)
    return jnp.dot(forward_normed + reverse_normed[::-1], w_out, precision=HIGHEST)
```

```python
import functools

import jax
import jax.numpy as jnp
from jax import lax
from jax.experimental import pallas as pl
from jax.experimental.pallas import tpu as pltpu
from jax.sharding import PartitionSpec as P

EPSILON = 1e-05
LOG2E = 1.4426950408889634
F32 = jnp.float32
BF = jnp.bfloat16
MESH = pl.DeviceIdType.MESH
NT = (((1,), (1,)), ((), ()))
TN = (((0,), (0,)), ((), ()))
NN = (((1,), (0,)), ((), ()))


def dot(a, b, dims=NN):
    return lax.dot_general(a, b, dims, preferred_element_type=F32)


def split2(x):
    hi = x.astype(BF)
    return hi, (x - hi.astype(F32)).astype(BF)


def split3(x):
    hi = x.astype(BF)
    rest = x - hi.astype(F32)
    mid = rest.astype(BF)
    return hi, mid, (rest - mid.astype(F32)).astype(BF)


def dot3(a, b, dims=NN):
    ah, al = split2(a)
    bh, bl = split2(b)
    return dot(ah, bh, dims) + dot(al, bh, dims) + dot(ah, bl, dims)


def silu(x):
    return x / (1.0 + jnp.exp(-x))


def rows_of(x, count):
    return jnp.broadcast_to(x, (count, x.shape[1]))


def kernel(
    n, ids_ref, comp_ref, emb_ref, wg_ref, wv_ref, ws_ref, wstep_ref, bias_ref, decay_ref,
    cv_ref, cs_ref, skip_ref, nw_ref, wo_ref, out_ref,
    ids_all, tab, wout, wbuf, wsbuf, ebc, sproj, taps_f, taps_r, cnt_all, oh_all,
    vtab, xs, xp, gate, gated, lrow, lsrc, went, skb, gmat, cmat, btab, accs,
    loc_sem, id_send, id_recv, tab_send, tab_recv, wo_send, wo_recv, wo_loc,
):
    me = lax.axis_index("ctx")
    tp = lax.axis_index("tp")
    other = 1 - tp
    block = ids_ref.shape[1]
    half = wg_ref.shape[1]
    depth = wg_ref.shape[0]
    rows = block // 2
    heads_half = bias_ref.shape[1]
    heads = 2 * heads_half
    state = ws_ref.shape[1] // 2
    inner = 2 * half
    total = n * block
    pairs = inner // 128
    chunk = half // 2

    loads = []
    for i in range(4):
        src = (wv_ref, wg_ref)[i // 2]
        loads.append(
            pltpu.make_async_copy(
                src.at[:, pl.ds((i % 2) * chunk, chunk)], wbuf.at[i], loc_sem.at[i]
            )
        )
    loads.append(pltpu.make_async_copy(ws_ref, wsbuf, loc_sem.at[4]))
    for load in loads:
        load.start()
    wo_copy = pltpu.make_async_copy(wo_ref, wout.at[tp], wo_loc)

    barrier = pltpu.get_barrier_semaphore()
    for d in range(1, n):
        pl.semaphore_signal(
            barrier, inc=1, device_id={"ctx": lax.rem(me + d, n)}, device_id_type=MESH
        )
    pl.semaphore_signal(barrier, inc=1, device_id={"tp": other}, device_id_type=MESH)
    ids_all[me] = ids_ref[...]
    pl.semaphore_wait(barrier, n)
    id_copies = []
    for d in range(1, n):
        copy = pltpu.make_async_remote_copy(
            src_ref=ids_ref, dst_ref=ids_all.at[me],
            send_sem=id_send.at[d - 1], recv_sem=id_recv.at[d - 1],
            device_id={"ctx": lax.rem(me + d, n)}, device_id_type=MESH,
        )
        copy.start()
        id_copies.append(copy)
    wo_remote = pltpu.make_async_remote_copy(
        src_ref=wo_ref, dst_ref=wout.at[tp], send_sem=wo_send, recv_sem=wo_recv,
        device_id={"tp": other}, device_id_type=MESH,
    )
    wo_remote.start()

    emb = jnp.concatenate([emb_ref[...], jnp.zeros((4, depth), F32)], axis=0)
    emb_t = jnp.transpose(jnp.concatenate([emb] * 16, axis=0))
    for v in range(4):
        ebc[v] = jnp.broadcast_to(emb_t[:, v : v + 1], (depth, 128))

    def project(ref, width):
        def body(i, accs_in):
            at = pl.ds(pl.multiple_of(i * 8, 8), 8)
            w = ref[at, :]
            new = []
            for v in range(4):
                e = ebc[v, at, :]
                e = jnp.concatenate([e] * (width // 128), axis=1) if width > 128 else e[:, :width]
                new.append(accs_in[v] + e * w)
            return tuple(new)

        start = tuple(jnp.zeros((8, width), F32) for _ in range(4))
        done = lax.fori_loop(0, depth // 8, body, start, unroll=8)
        return [jnp.sum(a, axis=0, keepdims=True) for a in done]

    for i in range(4):
        loads[i].wait()
        parts = project(wbuf.at[i], chunk)
        base = 8 if i < 2 else 0
        for v in range(4):
            tab[tp, pl.ds(base + v, 1), pl.ds((i % 2) * chunk, chunk)] = parts[v]
    tab[tp, 16:20, :] = cv_ref[...]
    tab[tp, 24:25, :] = nw_ref[...]
    raw = project(wstep_ref, heads_half)
    for v in range(4):
        z = raw[v] + bias_ref[...]
        step = jnp.maximum(z, 0.0) + jnp.log1p(jnp.exp(-jnp.abs(z)))
        tab[tp, 32 + v : 33 + v, 0:heads_half] = step
    tab[tp, 36:37, 0:heads_half] = decay_ref[...]
    tab[tp, 37:38, 0:heads_half] = skip_ref[...]
    tab_copy = pltpu.make_async_remote_copy(
        src_ref=tab.at[tp], dst_ref=tab.at[tp], send_sem=tab_send, recv_sem=tab_recv,
        device_id={"tp": other}, device_id_type=MESH,
    )
    tab_copy.start()
    loads[4].wait()
    parts = project(wsbuf, 2 * state)
    for v in range(4):
        sproj[v : v + 1, :] = parts[v]
    wo_copy.start()

    for copy in id_copies:
        copy.wait()
    null = 4
    lane = lax.broadcasted_iota(jnp.int32, (8, block), 1)
    sub = lax.broadcasted_iota(jnp.int32, (8, block), 0)
    tri = (
        lax.broadcasted_iota(jnp.int32, (block, block), 0)
        <= lax.broadcasted_iota(jnp.int32, (block, block), 1)
    ).astype(BF)
    comp = [comp_ref[v] for v in range(4)]
    first_row = me * block + tp * rows
    running = jnp.zeros((8, 1), F32)
    before = jnp.zeros((8, 1), F32)
    through = jnp.zeros((8, 1), F32)
    for j in range(n):
        own = ids_all[j]
        blank = jnp.full((1, 128), null, jnp.int32)
        left = ids_all[j - 1][:, block - 128 :] if j > 0 else blank
        right = ids_all[j + 1][:, :128] if j < n - 1 else blank
        ext = rows_of(jnp.concatenate([left, own, right], axis=1), 8)
        cext = jnp.full_like(ext, null)
        for v in range(4):
            cext = jnp.where(ext == v, comp[v], cext)
        width = block + 256
        fwd = [pltpu.roll(ext, 3 - k, 1)[:, 128 : 128 + block] if k < 3 else ext[:, 128 : 128 + block] for k in range(4)]
        rev = [
            pltpu.roll(cext, width - (3 - k), 1)[:, 128 : 128 + block] if k < 3 else cext[:, 128 : 128 + block]
            for k in range(4)
        ]
        def pack(taps):
            return jnp.where(sub == 0, taps[0], jnp.where(sub == 1, taps[1], jnp.where(sub == 2, taps[2], taps[3])))
        def code(taps):
            return 64 * taps[0] + 16 * taps[1] + 4 * taps[2] + taps[3]
        code_f, code_r = code(fwd), code(rev)
        if j == 0:
            code_f = jnp.where(lane < 3, 256 + lane, code_f)
        if j == n - 1:
            code_r = jnp.where(lane >= block - 3, 264 - block + lane, code_r)
        taps_f[j] = jnp.where(sub == 4, code_f, pack(fwd))
        taps_r[j] = jnp.where(sub == 4, code_r, pack(rev))
        oh = (fwd[3] == sub).astype(F32)
        counts = dot(oh.astype(BF), tri) + running
        cnt_all[j] = counts
        oh_all[j] = oh
        running = running + jnp.sum(oh, axis=1, keepdims=True)
        t = lane + j * block
        before = before + jnp.sum(jnp.where(t < first_row, oh, 0.0), axis=1, keepdims=True)
        through = through + jnp.sum(jnp.where(t < first_row + rows, oh, 0.0), axis=1, keepdims=True)

    tab_copy.wait()
    lane1 = lax.broadcasted_iota(jnp.int32, (8, 128), 1)
    par = jnp.where(
        lane1 < heads_half, tab[0, 32:40, 0:128], pltpu.roll(tab[1, 32:40, 0:128], heads_half, 1)
    )
    par_t = jnp.transpose(jnp.concatenate([par] * 16, axis=0))[:heads]
    step_f = [par_t[:, v : v + 1] for v in range(4)]
    decay = par_t[:, 4:5] * LOG2E
    skb[...] = jnp.broadcast_to(par_t[:, 5:6], (heads, 128))
    step_r = []
    for v in range(4):
        s = jnp.zeros_like(step_f[0])
        for u in range(4):
            s = s + jnp.where(comp[v] == u, 1.0, 0.0) * step_f[u]
        step_r.append(s)
    log_f = [-decay * s for s in step_f]
    log_r = [-decay * s for s in step_r]

    def mixv(cols, r):
        acc = cols[0] * r[0:1]
        for v in range(1, 4):
            acc = acc + cols[v] * r[v : v + 1]
        return acc

    tlane = lax.broadcasted_iota(jnp.int32, (heads, block), 1)
    centry = lax.broadcasted_iota(jnp.int32, (384, block), 0)
    wf = jnp.zeros((2 * heads, 384), F32)
    wr = jnp.zeros((2 * heads, 384), F32)
    for j in range(n):
        counts, oh = cnt_all[j], oh_all[j]
        t = tlane + j * block
        ef = jnp.where(t < first_row, mixv(log_f, before - counts), 0.0)
        er = jnp.where(t >= first_row + rows, mixv(log_r, counts - oh - through), 0.0)
        pf = jnp.where(t < first_row, jnp.exp2(ef) * mixv(step_f, oh), 0.0)
        pr = jnp.where(t >= first_row + rows, jnp.exp2(er) * mixv(step_r, oh), 0.0)
        hot_f = (centry == taps_f[j, 4:5, :]).astype(BF)
        hot_r = (centry == taps_r[j, 4:5, :]).astype(BF)
        wf = wf + dot(jnp.concatenate(split2(pf), axis=0), hot_f, NT)
        wr = wr + dot(jnp.concatenate(split2(pr), axis=0), hot_r, NT)
    went[0] = wf[:heads] + wf[heads:]
    went[1] = wr[:heads] + wr[heads:]

    local_at = pl.ds(pl.multiple_of(tp * rows, 128), rows)
    counts = cnt_all[me, :, local_at]
    oh = oh_all[me, :, local_at]
    l_f = mixv(log_f, counts - before)
    l_r = mixv(log_r, through - counts + oh)
    lrow[0] = l_f
    lrow[1] = l_r
    lsrc[0] = l_f - jnp.log2(mixv(step_f, oh))
    lsrc[1] = l_r - jnp.log2(mixv(step_r, oh))

    def hot16(taps, width):
        r = lax.broadcasted_iota(jnp.int32, (16, width), 0)
        k, v = r // 4, r % 4
        chosen = jnp.where(k == 0, taps[0], jnp.where(k == 1, taps[1], jnp.where(k == 2, taps[2], taps[3])))
        hot = jnp.where(chosen == v, 1.0, 0.0)
        return jnp.concatenate([hot, hot, hot], axis=0).astype(BF)

    tf = taps_f[me, :, local_at]
    tr = taps_r[me, :, local_at]
    hot_rows = [hot16([x[k : k + 1] for k in range(4)], rows) for x in (tf, tr)]
    codes = lax.broadcasted_iota(jnp.int32, (8, 256), 1)
    edge_f = taps_f[0, :, 0:128]
    edge_r = pltpu.roll(taps_r[n - 1, :, block - 128 :], 8, 1)
    edge = jnp.where(lane1 < 4, edge_f, edge_r)
    table_taps = []
    for k in range(4):
        digit = (codes[0:1] // (4 ** (3 - k))) % 4
        table_taps.append(jnp.concatenate([digit, edge[k : k + 1]], axis=1))
    hot_table = hot16(table_taps, 384)

    def tap_table(conv, proj):
        width = conv.shape[1]
        r = lax.broadcasted_iota(jnp.int32, (16, width), 0)
        k, v = r // 4, r % 4
        c = jnp.where(k == 0, conv[0:1], jnp.where(k == 1, conv[1:2], jnp.where(k == 2, conv[2:3], conv[3:4])))
        p = jnp.where(v == 0, proj[0:1], jnp.where(v == 1, proj[1:2], jnp.where(v == 2, proj[2:3], proj[3:4])))
        return jnp.concatenate(split3(c * p), axis=0)

    ct_state = tap_table(cs_ref[...], sproj[0:4, :])
    btab[...] = silu(dot(ct_state[:, :state], hot_table, TN))
    ri = lax.broadcasted_iota(jnp.int32, (rows, rows), 0)
    ci = lax.broadcasted_iota(jnp.int32, (rows, rows), 1)
    for s in range(2):
        maps = silu(dot(hot_rows[s], ct_state, TN))
        cmat[s] = maps[:, state:]
        seen = (ri >= ci) if s == 0 else (ri <= ci)
        gmat[s] = jnp.where(seen, dot3(maps[:, state:], maps[:, :state], NT), 0.0)

    own_hot = jnp.concatenate([oh[0:8]] * 3 + [jnp.zeros((24, rows), F32)], axis=0).astype(BF)
    rev_oh = jnp.zeros((8, rows), F32)
    sub_r = lax.broadcasted_iota(jnp.int32, (8, rows), 0)
    rev_oh = (tr[3:4] == sub_r).astype(F32)
    rev_hot = jnp.concatenate([rev_oh] * 3 + [jnp.zeros((24, rows), F32)], axis=0).astype(BF)
    for p in range(2):
        for q in range(4):
            width = half // 4
            lo = q * width
            at = slice(p * half + lo, p * half + lo + width)
            ct = tap_table(tab[p, 16:20, lo : lo + width], tab[p, 8:12, lo : lo + width])
            vtab[:, at] = silu(dot(hot_table, ct, TN))
            g8 = silu(tab[p, 0:8, lo : lo + width])
            r8 = lax.broadcasted_iota(jnp.int32, (8, width), 0)
            g8 = jnp.where(r8 < 4, g8, 0.0)
            gh, gm, gl = split3(g8)
            gt = jnp.concatenate(
                [gh.astype(F32), gm.astype(F32), gl.astype(F32), jnp.zeros((24, width), F32)], axis=0
            ).astype(BF)
            for s in range(2):
                xs[s, :, at] = silu(dot(hot_rows[s], ct, TN))
                gate[s, :, at] = dot((own_hot, rev_hot)[s], gt, TN)

    accs[...] = jnp.zeros_like(accs)
    low = lax.broadcasted_iota(jnp.int32, (rows, 128), 1) < 64
    low_c = lax.broadcasted_iota(jnp.int32, (384, 128), 1) < 64

    for s in range(2):
        c_hi, c_lo = split2(cmat[s])
        b_hi, b_lo = split2(btab[...])
        seen = (ri >= ci) if s == 0 else (ri <= ci)

        def pair(q, carry):
            at = pl.ds(pl.multiple_of(q * 128, 128), 128)
            x = xs[s, :, at]
            x_hi, x_lo = split2(x)
            both = jnp.concatenate([x_hi, x_lo], axis=1)
            ys, cols, ws = [], [], []
            for a in range(2):
                h = 2 * q + a
                col = jnp.transpose(rows_of(lrow[s, pl.ds(h, 1), :], 128))
                wide = jnp.concatenate([col] * (rows // 128), axis=1)
                e = jnp.where(seen, wide - lsrc[s, pl.ds(h, 1), :], -1e30)
                d_hi, d_lo = split2(jnp.exp2(e) * gmat[s])
                r = dot(d_hi, both)
                ys.append(r[:, :128] + r[:, 128:] + dot(d_lo, x_hi))
                cols.append(col)
                ws.append(jnp.transpose(rows_of(went[s, pl.ds(h, 1), :], 128)))
            y = jnp.where(low, ys[0], ys[1])
            vw_hi, vw_lo = split2(vtab[:, at] * jnp.where(low_c, ws[0], ws[1]))
            mem = dot(b_hi, vw_hi) + dot(b_lo, vw_hi) + dot(b_hi, vw_lo)
            m_hi, m_lo = split2(mem)
            carried = dot(c_hi, m_hi) + dot(c_lo, m_hi) + dot(c_hi, m_lo)
            y = y + carried * jnp.exp2(jnp.where(low, cols[0], cols[1]))
            sk = jnp.where(low[0:1], skb[pl.ds(2 * q, 1), :], skb[pl.ds(2 * q + 1, 1), :])
            g = (y + sk * x) * gate[s, :, at]
            gated[s, :, at] = g
            accs[s] = accs[s] + g * g
            return carry

        lax.fori_loop(0, pairs, pair, 0)

    scales = [
        lax.rsqrt(jnp.sum(accs[s], axis=1, keepdims=True) / inner + EPSILON) for s in range(2)
    ]
    wo_copy.wait()
    wo_remote.wait()
    out_ref[...] = jnp.zeros_like(out_ref)
    step_k = 256
    for p in range(2):
        def project_out(q, carry):
            lo = pl.multiple_of(q * step_k, step_k)
            at = pl.ds(pl.multiple_of(p * half + q * step_k, step_k), step_k)
            mixed = (gated[0, :, at] * scales[0] + gated[1, :, at] * scales[1]) * tab[
                p, 24:25, pl.ds(lo, step_k)
            ]
            out_ref[...] += dot3(mixed, wout[p, pl.ds(lo, step_k), :])
            return carry

        lax.fori_loop(0, half // step_k, project_out, 0)


def local(
    nucleotides, complement, embedding, w_gate, w_value, w_state, w_step, step_bias,
    decay_rate, conv_value, conv_state, skip_gain, norm_weight, w_out,
):
    n = lax.axis_size("ctx")
    block = nucleotides.shape[0]
    rows = block // 2
    half = w_gate.shape[1]
    depth = w_gate.shape[0]
    inner = 2 * half
    heads = 2 * step_bias.shape[0]
    state = w_state.shape[1] // 2
    vm = pl.BlockSpec(memory_space=pltpu.VMEM)
    hbm = pl.BlockSpec(memory_space=pl.ANY)
    sm = pl.BlockSpec(memory_space=pltpu.SMEM)
    dma = pltpu.SemaphoreType.DMA
    return pl.pallas_call(
        functools.partial(kernel, n),
        out_shape=jax.ShapeDtypeStruct((rows, w_out.shape[1]), F32),
        in_specs=[vm, sm, vm, hbm, hbm, hbm, vm, vm, vm, vm, vm, vm, vm, hbm],
        out_specs=vm,
        scratch_shapes=[
            pltpu.VMEM((n, 1, block), jnp.int32),
            pltpu.VMEM((2, 40, half), F32),
            pltpu.VMEM((2, half, w_out.shape[1]), F32),
            pltpu.VMEM((4, depth, half // 2), F32),
            pltpu.VMEM((depth, 2 * state), F32),
            pltpu.VMEM((4, depth, 128), F32),
            pltpu.VMEM((8, 2 * state), F32),
            pltpu.VMEM((n, 8, block), jnp.int32),
            pltpu.VMEM((n, 8, block), jnp.int32),
            pltpu.VMEM((n, 8, block), F32),
            pltpu.VMEM((n, 8, block), F32),
            pltpu.VMEM((384, inner), F32),
            pltpu.VMEM((2, rows, inner), F32),
            pltpu.VMEM((8, 128), F32),
            pltpu.VMEM((2, rows, inner), F32),
            pltpu.VMEM((2, rows, inner), F32),
            pltpu.VMEM((2, heads, rows), F32),
            pltpu.VMEM((2, heads, rows), F32),
            pltpu.VMEM((2, heads, 384), F32),
            pltpu.VMEM((heads, 128), F32),
            pltpu.VMEM((2, rows, rows), F32),
            pltpu.VMEM((2, rows, state), F32),
            pltpu.VMEM((state, 384), F32),
            pltpu.VMEM((2, rows, 128), F32),
            dma((5,)),
            dma((n - 1,)),
            dma((n - 1,)),
            dma, dma, dma, dma, dma,
        ],
        compiler_params=pltpu.CompilerParams(
            collective_id=0, has_side_effects=True, vmem_limit_bytes=60 * 1024 * 1024
        ),
    )(
        nucleotides[None, :], complement, embedding, w_gate, w_value, w_state, w_step,
        step_bias[None, :], decay_rate[None, :], conv_value, conv_state, skip_gain[None, :],
        norm_weight[None, :], w_out,
    )


def solution(mesh):
    placed = (
        P(("dp", "ctx")), P(), P(), P(None, "tp"), P(None, "tp"), P(), P(None, "tp"),
        P("tp"), P("tp"), P(None, "tp"), P(), P("tp"), P("tp"), P("tp", None),
    )
    return jax.shard_map(
        local, mesh=mesh, in_specs=placed, out_specs=P(("dp", "ctx", "tp"), None), check_vma=False
    )
```

```python
import functools

import jax
import jax.numpy as jnp
from jax import lax
from jax.experimental import pallas as pl
from jax.experimental.pallas import tpu as pltpu
from jax.sharding import PartitionSpec as P

EPSILON = 1e-05
LOG2E = 1.4426950408889634
F32 = jnp.float32
BF = jnp.bfloat16
MESH = pl.DeviceIdType.MESH
NT = (((1,), (1,)), ((), ()))
TN = (((0,), (0,)), ((), ()))
NN = (((1,), (0,)), ((), ()))


def dot(a, b, dims=NN):
    return lax.dot_general(a, b, dims, preferred_element_type=F32)


def split2(x):
    hi = x.astype(BF)
    return hi, (x - hi.astype(F32)).astype(BF)


def split3(x):
    hi = x.astype(BF)
    rest = x - hi.astype(F32)
    mid = rest.astype(BF)
    return hi, mid, (rest - mid.astype(F32)).astype(BF)


def dot3(a, b, dims=NN):
    ah, al = split2(a)
    bh, bl = split2(b)
    return dot(ah, bh, dims) + dot(al, bh, dims) + dot(ah, bl, dims)


def silu(x):
    half = 0.5 * x
    return half + half * jnp.tanh(half)


def rows_of(x, count):
    return jnp.broadcast_to(x, (count, x.shape[1]))


def kernel(
    n, ids_ref, comp_ref, emb_ref, wg_ref, wv_ref, ws_ref, wstep_ref, bias_ref, decay_ref,
    cv_ref, cs_ref, skip_ref, nw_ref, wo_ref, out_ref,
    ids_all, tab, wout, wbuf, wsbuf, ebc, sproj, taps_f, taps_r, cnt_all, oh_all,
    vtab, xs, xp, gate, gated, lrow, lsrc, went, skb, gmat, cmat, btab, accs, ccat, bcat, becat,
    loc_sem, id_send, id_recv, tab_send, tab_recv, wo_send, wo_recv, wo_loc,
):
    me = lax.axis_index("ctx")
    tp = lax.axis_index("tp")
    other = 1 - tp
    block = ids_ref.shape[1]
    half = wg_ref.shape[1]
    depth = wg_ref.shape[0]
    rows = block // 2
    heads_half = bias_ref.shape[1]
    heads = 2 * heads_half
    state = ws_ref.shape[1] // 2
    inner = 2 * half
    total = n * block
    pairs = inner // 128
    chunk = half // 2

    loads = []
    for i in range(4):
        src = (wv_ref, wg_ref)[i // 2]
        loads.append(
            pltpu.make_async_copy(
                src.at[:, pl.ds((i % 2) * chunk, chunk)], wbuf.at[i], loc_sem.at[i]
            )
        )
    loads.append(pltpu.make_async_copy(ws_ref, wsbuf, loc_sem.at[4]))
    for load in loads:
        load.start()
    wo_copy = pltpu.make_async_copy(wo_ref, wout.at[tp], wo_loc)

    barrier = pltpu.get_barrier_semaphore()
    for d in range(1, n):
        pl.semaphore_signal(
            barrier, inc=1, device_id={"ctx": lax.rem(me + d, n)}, device_id_type=MESH
        )
    pl.semaphore_signal(barrier, inc=1, device_id={"tp": other}, device_id_type=MESH)
    ids_all[me] = ids_ref[...]
    pl.semaphore_wait(barrier, n)
    id_copies = []
    for d in range(1, n):
        copy = pltpu.make_async_remote_copy(
            src_ref=ids_ref, dst_ref=ids_all.at[me],
            send_sem=id_send.at[d - 1], recv_sem=id_recv.at[d - 1],
            device_id={"ctx": lax.rem(me + d, n)}, device_id_type=MESH,
        )
        copy.start()
        id_copies.append(copy)
    wo_remote = pltpu.make_async_remote_copy(
        src_ref=wo_ref, dst_ref=wout.at[tp], send_sem=wo_send, recv_sem=wo_recv,
        device_id={"tp": other}, device_id_type=MESH,
    )
    wo_remote.start()

    emb = jnp.concatenate([emb_ref[...], jnp.zeros((4, depth), F32)], axis=0)
    emb_t = jnp.transpose(jnp.concatenate([emb] * 16, axis=0))
    for v in range(4):
        ebc[v] = jnp.broadcast_to(emb_t[:, v : v + 1], (depth, 128))

    def project(ref, width):
        def body(i, accs_in):
            at = pl.ds(pl.multiple_of(i * 8, 8), 8)
            w = ref[at, :]
            new = []
            for v in range(4):
                e = ebc[v, at, :]
                e = jnp.concatenate([e] * (width // 128), axis=1) if width > 128 else e[:, :width]
                new.append(accs_in[v] + e * w)
            return tuple(new)

        start = tuple(jnp.zeros((8, width), F32) for _ in range(4))
        done = lax.fori_loop(0, depth // 8, body, start, unroll=8)
        return [jnp.sum(a, axis=0, keepdims=True) for a in done]

    for i in range(4):
        loads[i].wait()
        parts = project(wbuf.at[i], chunk)
        base = 8 if i < 2 else 0
        for v in range(4):
            tab[tp, pl.ds(base + v, 1), pl.ds((i % 2) * chunk, chunk)] = parts[v]
    tab[tp, 16:20, :] = cv_ref[...]
    tab[tp, 24:25, :] = nw_ref[...]
    for v in range(4):
        z = jnp.sum(wstep_ref[...] * emb_ref[v : v + 1, :], axis=1, keepdims=True)
        xp[:, v : v + 1] = z
    raw = jnp.transpose(jnp.concatenate([xp[...]] * (128 // heads_half), axis=0))
    z = raw[0:8, 0:heads_half] + bias_ref[...]
    step = jnp.maximum(z, 0.0) + jnp.log1p(jnp.exp(-jnp.abs(z)))
    tab[tp, 32:36, 0:heads_half] = step[0:4]
    tab[tp, 36:37, 0:heads_half] = decay_ref[...]
    tab[tp, 37:38, 0:heads_half] = skip_ref[...]
    tab_copy = pltpu.make_async_remote_copy(
        src_ref=tab.at[tp], dst_ref=tab.at[tp], send_sem=tab_send, recv_sem=tab_recv,
        device_id={"tp": other}, device_id_type=MESH,
    )
    tab_copy.start()
    loads[4].wait()
    parts = project(wsbuf, 2 * state)
    for v in range(4):
        sproj[v : v + 1, :] = parts[v]
    wo_copy.start()

    for copy in id_copies:
        copy.wait()
    null = 4
    lane = lax.broadcasted_iota(jnp.int32, (8, block), 1)
    sub = lax.broadcasted_iota(jnp.int32, (8, block), 0)
    tri = (
        lax.broadcasted_iota(jnp.int32, (block, block), 0)
        <= lax.broadcasted_iota(jnp.int32, (block, block), 1)
    ).astype(BF)
    comp = [comp_ref[v] for v in range(4)]
    first_row = me * block + tp * rows
    running = jnp.zeros((8, 1), F32)
    before = jnp.zeros((8, 1), F32)
    through = jnp.zeros((8, 1), F32)
    for j in range(n):
        own = ids_all[j]
        blank = jnp.full((1, 128), null, jnp.int32)
        left = ids_all[j - 1][:, block - 128 :] if j > 0 else blank
        right = ids_all[j + 1][:, :128] if j < n - 1 else blank
        ext = rows_of(jnp.concatenate([left, own, right], axis=1), 8)
        cext = jnp.full_like(ext, null)
        for v in range(4):
            cext = jnp.where(ext == v, comp[v], cext)
        width = block + 256
        fwd = [pltpu.roll(ext, 3 - k, 1)[:, 128 : 128 + block] if k < 3 else ext[:, 128 : 128 + block] for k in range(4)]
        rev = [
            pltpu.roll(cext, width - (3 - k), 1)[:, 128 : 128 + block] if k < 3 else cext[:, 128 : 128 + block]
            for k in range(4)
        ]
        def pack(taps):
            return jnp.where(sub == 0, taps[0], jnp.where(sub == 1, taps[1], jnp.where(sub == 2, taps[2], taps[3])))
        def code(taps):
            return 64 * taps[0] + 16 * taps[1] + 4 * taps[2] + taps[3]
        code_f, code_r = code(fwd), code(rev)
        if j == 0:
            code_f = jnp.where(lane < 3, 256 + lane, code_f)
        if j == n - 1:
            code_r = jnp.where(lane >= block - 3, 264 - block + lane, code_r)
        taps_f[j] = jnp.where(sub == 4, code_f, pack(fwd))
        taps_r[j] = jnp.where(sub == 4, code_r, pack(rev))
        oh = (fwd[3] == sub).astype(F32)
        counts = dot(oh.astype(BF), tri) + running
        cnt_all[j] = counts
        oh_all[j] = oh
        running = running + jnp.sum(oh, axis=1, keepdims=True)
        t = lane + j * block
        before = before + jnp.sum(jnp.where(t < first_row, oh, 0.0), axis=1, keepdims=True)
        through = through + jnp.sum(jnp.where(t < first_row + rows, oh, 0.0), axis=1, keepdims=True)

    tab_copy.wait()
    lane1 = lax.broadcasted_iota(jnp.int32, (8, 128), 1)
    par = jnp.where(
        lane1 < heads_half, tab[0, 32:40, 0:128], pltpu.roll(tab[1, 32:40, 0:128], heads_half, 1)
    )
    par_t = jnp.transpose(jnp.concatenate([par] * 16, axis=0))[:heads]
    step_f = [par_t[:, v : v + 1] for v in range(4)]
    decay = par_t[:, 4:5] * LOG2E
    skb[...] = jnp.broadcast_to(par_t[:, 5:6], (heads, 128))
    step_r = []
    for v in range(4):
        s = jnp.zeros_like(step_f[0])
        for u in range(4):
            s = s + jnp.where(comp[v] == u, 1.0, 0.0) * step_f[u]
        step_r.append(s)
    log_f = [-decay * s for s in step_f]
    log_r = [-decay * s for s in step_r]

    def mixv(cols, r):
        acc = cols[0] * r[0:1]
        for v in range(1, 4):
            acc = acc + cols[v] * r[v : v + 1]
        return acc

    tlane = lax.broadcasted_iota(jnp.int32, (heads, block), 1)
    centry = lax.broadcasted_iota(jnp.int32, (384, block), 0)
    wf = jnp.zeros((2 * heads, 384), F32)
    wr = jnp.zeros((2 * heads, 384), F32)
    for j in range(n):
        counts, oh = cnt_all[j], oh_all[j]
        t = tlane + j * block
        ef = jnp.where(t < first_row, mixv(log_f, before - counts), 0.0)
        er = jnp.where(t >= first_row + rows, mixv(log_r, counts - oh - through), 0.0)
        pf = jnp.where(t < first_row, jnp.exp2(ef) * mixv(step_f, oh), 0.0)
        pr = jnp.where(t >= first_row + rows, jnp.exp2(er) * mixv(step_r, oh), 0.0)
        hot_f = (centry == taps_f[j, 4:5, :]).astype(BF)
        hot_r = (centry == taps_r[j, 4:5, :]).astype(BF)
        wf = wf + dot(jnp.concatenate(split2(pf), axis=0), hot_f, NT)
        wr = wr + dot(jnp.concatenate(split2(pr), axis=0), hot_r, NT)
    went[0] = wf[:heads] + wf[heads:]
    went[1] = wr[:heads] + wr[heads:]

    local_at = pl.ds(pl.multiple_of(tp * rows, 128), rows)
    counts = cnt_all[me, :, local_at]
    oh = oh_all[me, :, local_at]
    l_f = mixv(log_f, counts - before)
    l_r = mixv(log_r, through - counts + oh)
    lrow[0] = l_f
    lrow[1] = l_r
    lsrc[0] = l_f - jnp.log2(mixv(step_f, oh))
    lsrc[1] = l_r - jnp.log2(mixv(step_r, oh))

    def hot16(taps, width):
        r = lax.broadcasted_iota(jnp.int32, (16, width), 0)
        k, v = r // 4, r % 4
        chosen = jnp.where(k == 0, taps[0], jnp.where(k == 1, taps[1], jnp.where(k == 2, taps[2], taps[3])))
        hot = jnp.where(chosen == v, 1.0, 0.0)
        return jnp.concatenate([hot, hot, hot], axis=0).astype(BF)

    tf = taps_f[me, :, local_at]
    tr = taps_r[me, :, local_at]
    hot_rows = [hot16([x[k : k + 1] for k in range(4)], rows) for x in (tf, tr)]
    codes = lax.broadcasted_iota(jnp.int32, (8, 256), 1)
    edge_f = taps_f[0, :, 0:128]
    edge_r = pltpu.roll(taps_r[n - 1, :, block - 128 :], 8, 1)
    edge = jnp.where(lane1 < 4, edge_f, edge_r)
    table_taps = []
    for k in range(4):
        digit = (codes[0:1] // (4 ** (3 - k))) % 4
        table_taps.append(jnp.concatenate([digit, edge[k : k + 1]], axis=1))
    hot_table = hot16(table_taps, 384)

    def tap_table(conv, proj):
        width = conv.shape[1]
        r = lax.broadcasted_iota(jnp.int32, (16, width), 0)
        k, v = r // 4, r % 4
        c = jnp.where(k == 0, conv[0:1], jnp.where(k == 1, conv[1:2], jnp.where(k == 2, conv[2:3], conv[3:4])))
        p = jnp.where(v == 0, proj[0:1], jnp.where(v == 1, proj[1:2], jnp.where(v == 2, proj[2:3], proj[3:4])))
        return jnp.concatenate(split3(c * p), axis=0)

    ct_state = tap_table(cs_ref[...], sproj[0:4, :])
    btab[...] = silu(dot(ct_state[:, :state], hot_table, TN))
    ri = lax.broadcasted_iota(jnp.int32, (rows, rows), 0)
    ci = lax.broadcasted_iota(jnp.int32, (rows, rows), 1)
    for s in range(2):
        maps = silu(dot(hot_rows[s], ct_state, TN))
        cmat[s] = maps[:, state:]
        seen = (ri >= ci) if s == 0 else (ri <= ci)
        gmat[s] = jnp.where(seen, dot3(maps[:, state:], maps[:, :state], NT), 0.0)

    own_hot = jnp.concatenate([oh[0:8]] * 3 + [jnp.zeros((24, rows), F32)], axis=0).astype(BF)
    rev_oh = jnp.zeros((8, rows), F32)
    sub_r = lax.broadcasted_iota(jnp.int32, (8, rows), 0)
    rev_oh = (tr[3:4] == sub_r).astype(F32)
    rev_hot = jnp.concatenate([rev_oh] * 3 + [jnp.zeros((24, rows), F32)], axis=0).astype(BF)
    for p in range(2):
        for q in range(4):
            width = half // 4
            lo = q * width
            at = slice(p * half + lo, p * half + lo + width)
            ct = tap_table(tab[p, 16:20, lo : lo + width], tab[p, 8:12, lo : lo + width])
            vtab[0:256, at] = silu(dot(hot_table[:, :256], ct, TN))
            vtab[256:272, at] = silu(dot(hot_table[:, 256:], ct, TN)[:16])
            g8 = silu(tab[p, 0:8, lo : lo + width])
            r8 = lax.broadcasted_iota(jnp.int32, (8, width), 0)
            g8 = jnp.where(r8 < 4, g8, 0.0)
            gh, gm, gl = split3(g8)
            gt = jnp.concatenate(
                [gh.astype(F32), gm.astype(F32), gl.astype(F32), jnp.zeros((24, width), F32)], axis=0
            ).astype(BF)
            for s in range(2):
                xs[s, :, at] = silu(dot(hot_rows[s], ct, TN))
                gate[s, :, at] = dot((own_hot, rev_hot)[s], gt, TN)

    accs[...] = jnp.zeros_like(accs)
    mid = rows // 2
    low = lax.broadcasted_iota(jnp.int32, (rows, 128), 1) < 64
    tri_r = lax.broadcasted_iota(jnp.int32, (mid, mid), 0)
    tri_c = lax.broadcasted_iota(jnp.int32, (mid, mid), 1)
    for s in range(2):
        ccat[s] = jnp.concatenate(split2(cmat[s]), axis=1)
    b_hi, b_lo = split2(btab[...])
    bcat[...] = jnp.concatenate([b_hi[:, :256], b_lo[:, :256]], axis=0)
    e_hi = b_hi[:, 256:].astype(F32)
    e_lo = pltpu.roll(b_lo[:, 256:].astype(F32), 16, 1)
    elane = lax.broadcasted_iota(jnp.int32, (state, 128), 1)
    becat[...] = jnp.where(elane < 16, e_hi, jnp.where(elane < 32, e_lo, 0.0)).astype(BF)

    def heads_rows(ref, s, h, at):
        return jnp.concatenate(
            [rows_of(ref[s, pl.ds(h, 1), :][:, at], 64), rows_of(ref[s, pl.ds(h + 1, 1), :][:, at], 64)], axis=0
        )

    def pair(q, carry):
        at = pl.ds(pl.multiple_of(q * 128, 128), 128)
        vt, ve = vtab[0:256, at], vtab[256:272, at]
        sk = jnp.where(low[0:1], skb[pl.ds(2 * q, 1), :], skb[pl.ds(2 * q + 1, 1), :])
        for s in range(2):
            near = slice(0, mid) if s == 0 else slice(mid, rows)
            far = slice(mid, rows) if s == 0 else slice(0, mid)
            seen = (tri_r >= tri_c) if s == 0 else (tri_r <= tri_c)
            x = xs[s, :, at]
            x_hi, x_lo = split2(x)
            both = jnp.concatenate([x_hi, x_lo], axis=1)
            near_both = jnp.concatenate([both[near], both[near]], axis=0)
            near_l, far_hi, far_lo, cols = [], [], [], []
            for a in range(2):
                h = 2 * q + a
                col = jnp.transpose(rows_of(lrow[s, pl.ds(h, 1), :], 128))
                src = lsrc[s, pl.ds(h, 1), :]
                def decayed(i, j, masked):
                    e = col[i] - src[:, j]
                    if masked:
                        e = jnp.where(seen, e, -1e30)
                    return split2(jnp.exp2(e) * gmat[s, i, j])
                nn_hi, nn_lo = decayed(near, near, True)
                ff_hi, ff_lo = decayed(far, far, True)
                fn_hi, fn_lo = decayed(far, near, False)
                near_l.append(jnp.concatenate([nn_hi, nn_lo], axis=1))
                order = (fn_hi, ff_hi) if s == 0 else (ff_hi, fn_hi)
                far_hi.append(jnp.concatenate(order, axis=1))
                order = (fn_lo, ff_lo) if s == 0 else (ff_lo, fn_lo)
                far_lo.append(jnp.concatenate(order, axis=1))
                cols.append(col)
            rn = dot(jnp.concatenate(near_l, axis=0), near_both)
            rf = dot(jnp.concatenate(far_hi, axis=0), both)
            rl = dot(jnp.concatenate(far_lo, axis=0), x_hi)
            rn = rn[:, :128] + rn[:, 128:]
            rf = rf[:, :128] + rf[:, 128:] + rl
            lowm = low[:mid]
            yn = jnp.where(lowm, rn[:mid], rn[mid:])
            yf = jnp.where(lowm, rf[:mid], rf[mid:])
            y = jnp.concatenate([yn, yf] if s == 0 else [yf, yn], axis=0)
            w = jnp.transpose(heads_rows(went, s, 2 * q, slice(0, 256)))
            we = jnp.transpose(heads_rows(went, s, 2 * q, slice(256, 384)))[:16]
            vw = jnp.concatenate(split2(vt * w), axis=1)
            vwe = jnp.concatenate(split2(ve * we), axis=1)
            vwe = jnp.concatenate([vwe, vwe], axis=0)
            r = dot(bcat[...], vw)
            r = r[:state] + r[state:] + dot(becat[:, 0:32], vwe)
            mem = r[:, :128] + r[:, 128:]
            m2 = jnp.concatenate(split2(mem), axis=1)
            carried = dot(ccat[s], jnp.concatenate([m2, m2], axis=0))
            carried = carried[:, :128] + carried[:, 128:]
            y = y + carried * jnp.exp2(jnp.where(low, cols[0], cols[1]))
            g = (y + sk * x) * gate[s, :, at]
            gated[s, :, at] = g
            accs[s] = accs[s] + g * g
        return carry

    lax.fori_loop(0, pairs, pair, 0)

    scales = [
        lax.rsqrt(jnp.sum(accs[s], axis=1, keepdims=True) / inner + EPSILON) for s in range(2)
    ]
    wo_copy.wait()
    wo_remote.wait()
    out_ref[...] = jnp.zeros_like(out_ref)
    step_k = 256
    for p in range(2):
        def project_out(q, carry):
            lo = pl.multiple_of(q * step_k, step_k)
            at = pl.ds(pl.multiple_of(p * half + q * step_k, step_k), step_k)
            mixed = (gated[0, :, at] * scales[0] + gated[1, :, at] * scales[1]) * tab[
                p, 24:25, pl.ds(lo, step_k)
            ]
            out_ref[...] += dot3(mixed, wout[p, pl.ds(lo, step_k), :])
            return carry

        lax.fori_loop(0, half // step_k, project_out, 0)


def local(
    nucleotides, complement, embedding, w_gate, w_value, w_state, w_step, step_bias,
    decay_rate, conv_value, conv_state, skip_gain, norm_weight, w_out,
):
    n = lax.axis_size("ctx")
    block = nucleotides.shape[0]
    rows = block // 2
    half = w_gate.shape[1]
    depth = w_gate.shape[0]
    inner = 2 * half
    heads = 2 * step_bias.shape[0]
    state = w_state.shape[1] // 2
    vm = pl.BlockSpec(memory_space=pltpu.VMEM)
    hbm = pl.BlockSpec(memory_space=pl.ANY)
    sm = pl.BlockSpec(memory_space=pltpu.SMEM)
    dma = pltpu.SemaphoreType.DMA
    return pl.pallas_call(
        functools.partial(kernel, n),
        out_shape=jax.ShapeDtypeStruct((rows, w_out.shape[1]), F32),
        in_specs=[vm, sm, vm, hbm, hbm, hbm, vm, vm, vm, vm, vm, vm, vm, hbm],
        out_specs=vm,
        scratch_shapes=[
            pltpu.VMEM((n, 1, block), jnp.int32),
            pltpu.VMEM((2, 40, half), F32),
            pltpu.VMEM((2, half, w_out.shape[1]), F32),
            pltpu.VMEM((4, depth, half // 2), F32),
            pltpu.VMEM((depth, 2 * state), F32),
            pltpu.VMEM((4, depth, 128), F32),
            pltpu.VMEM((8, 2 * state), F32),
            pltpu.VMEM((n, 8, block), jnp.int32),
            pltpu.VMEM((n, 8, block), jnp.int32),
            pltpu.VMEM((n, 8, block), F32),
            pltpu.VMEM((n, 8, block), F32),
            pltpu.VMEM((272, inner), F32),
            pltpu.VMEM((2, rows, inner), F32),
            pltpu.VMEM((heads // 2, 128), F32),
            pltpu.VMEM((2, rows, inner), F32),
            pltpu.VMEM((2, rows, inner), F32),
            pltpu.VMEM((2, heads, rows), F32),
            pltpu.VMEM((2, heads, rows), F32),
            pltpu.VMEM((2, heads, 384), F32),
            pltpu.VMEM((heads, 128), F32),
            pltpu.VMEM((2, rows, rows), F32),
            pltpu.VMEM((2, rows, state), F32),
            pltpu.VMEM((state, 384), F32),
            pltpu.VMEM((2, rows, 128), F32),
            pltpu.VMEM((2, rows, 2 * state), BF),
            pltpu.VMEM((2 * state, 256), BF),
            pltpu.VMEM((state, 128), BF),
            dma((5,)),
            dma((n - 1,)),
            dma((n - 1,)),
            dma, dma, dma, dma, dma,
        ],
        compiler_params=pltpu.CompilerParams(
            collective_id=0, has_side_effects=True, vmem_limit_bytes=60 * 1024 * 1024
        ),
    )(
        nucleotides[None, :], complement, embedding, w_gate, w_value, w_state, w_step.T,
        step_bias[None, :], decay_rate[None, :], conv_value, conv_state, skip_gain[None, :],
        norm_weight[None, :], w_out,
    )


def solution(mesh):
    placed = (
        P(("dp", "ctx")), P(), P(), P(None, "tp"), P(None, "tp"), P(), P(None, "tp"),
        P("tp"), P("tp"), P(None, "tp"), P(), P("tp"), P("tp"), P("tp", None),
    )
    return jax.shard_map(
        local, mesh=mesh, in_specs=placed, out_specs=P(("dp", "ctx", "tp"), None), check_vma=False
    )
```

```python
import functools

import jax
import jax.numpy as jnp
from jax import lax
from jax.experimental import pallas as pl
from jax.experimental.pallas import tpu as pltpu
from jax.sharding import PartitionSpec as P

EPSILON = 1e-05
LOG2E = 1.4426950408889634
F32 = jnp.float32
BF = jnp.bfloat16
MESH = pl.DeviceIdType.MESH
NT = (((1,), (1,)), ((), ()))
TN = (((0,), (0,)), ((), ()))
NN = (((1,), (0,)), ((), ()))


def dot(a, b, dims=NN):
    return lax.dot_general(a, b, dims, preferred_element_type=F32)


def split2(x):
    hi = x.astype(BF)
    return hi, (x - hi.astype(F32)).astype(BF)


def split3(x):
    hi = x.astype(BF)
    rest = x - hi.astype(F32)
    mid = rest.astype(BF)
    return hi, mid, (rest - mid.astype(F32)).astype(BF)


def dot3(a, b, dims=NN):
    ah, al = split2(a)
    bh, bl = split2(b)
    return dot(ah, bh, dims) + dot(al, bh, dims) + dot(ah, bl, dims)


def silu(x):
    half = 0.5 * x
    return half + half * jnp.tanh(half)


def rows_of(x, count):
    return jnp.broadcast_to(x, (count, x.shape[1]))


def kernel(
    n, ids_ref, comp_ref, emb_ref, wg_ref, wv_ref, ws_ref, wstep_ref, bias_ref, decay_ref,
    cv_ref, cs_ref, skip_ref, nw_ref, wo_ref, out_ref,
    ids_all, tab, wout, wbuf, wsbuf, ebc, sproj, taps_f, taps_r, cnt_all, oh_all,
    vtab, xs, xp, gate, gated, lrow, lsrc, went, skb, gmat, cmat, btab, accs, ccat, bcat, becat,
    loc_sem, id_send, id_recv, tab_send, tab_recv, wo_send, wo_recv, wo_loc,
):
    me = lax.axis_index("ctx")
    tp = lax.axis_index("tp")
    other = 1 - tp
    block = ids_ref.shape[1]
    half = wg_ref.shape[1]
    depth = wg_ref.shape[0]
    rows = block // 2
    heads_half = bias_ref.shape[1]
    heads = 2 * heads_half
    state = ws_ref.shape[1] // 2
    inner = 2 * half
    total = n * block
    pairs = inner // 128
    chunk = half // 2

    loads = []
    for i in range(4):
        src = (wv_ref, wg_ref)[i // 2]
        loads.append(
            pltpu.make_async_copy(
                src.at[:, pl.ds((i % 2) * chunk, chunk)], wbuf.at[i], loc_sem.at[i]
            )
        )
    loads.append(pltpu.make_async_copy(ws_ref, wsbuf, loc_sem.at[4]))
    for load in loads:
        load.start()
    wo_copy = pltpu.make_async_copy(wo_ref, wout.at[tp], wo_loc)

    barrier = pltpu.get_barrier_semaphore()
    for d in range(1, n):
        pl.semaphore_signal(
            barrier, inc=1, device_id={"ctx": lax.rem(me + d, n)}, device_id_type=MESH
        )
    pl.semaphore_signal(barrier, inc=1, device_id={"tp": other}, device_id_type=MESH)
    ids_all[me] = ids_ref[...]
    pl.semaphore_wait(barrier, n)
    id_copies = []
    for d in range(1, n):
        copy = pltpu.make_async_remote_copy(
            src_ref=ids_ref, dst_ref=ids_all.at[me],
            send_sem=id_send.at[d - 1], recv_sem=id_recv.at[d - 1],
            device_id={"ctx": lax.rem(me + d, n)}, device_id_type=MESH,
        )
        copy.start()
        id_copies.append(copy)
    wo_remote = pltpu.make_async_remote_copy(
        src_ref=wo_ref, dst_ref=wout.at[tp], send_sem=wo_send, recv_sem=wo_recv,
        device_id={"tp": other}, device_id_type=MESH,
    )
    wo_remote.start()

    emb = jnp.concatenate([emb_ref[...], jnp.zeros((4, depth), F32)], axis=0)
    emb_t = jnp.transpose(jnp.concatenate([emb] * 16, axis=0))
    for v in range(4):
        ebc[v] = jnp.broadcast_to(emb_t[:, v : v + 1], (depth, 128))

    def project(ref, width):
        def body(i, accs_in):
            at = pl.ds(pl.multiple_of(i * 8, 8), 8)
            w = ref[at, :]
            new = []
            for v in range(4):
                e = ebc[v, at, :]
                e = jnp.concatenate([e] * (width // 128), axis=1) if width > 128 else e[:, :width]
                new.append(accs_in[v] + e * w)
            return tuple(new)

        start = tuple(jnp.zeros((8, width), F32) for _ in range(4))
        done = lax.fori_loop(0, depth // 8, body, start, unroll=8)
        return [jnp.sum(a, axis=0, keepdims=True) for a in done]

    for i in range(4):
        loads[i].wait()
        parts = project(wbuf.at[i], chunk)
        base = 8 if i < 2 else 0
        for v in range(4):
            tab[tp, pl.ds(base + v, 1), pl.ds((i % 2) * chunk, chunk)] = parts[v]
    tab[tp, 16:20, :] = cv_ref[...]
    tab[tp, 24:25, :] = nw_ref[...]
    for v in range(4):
        z = jnp.sum(wstep_ref[...] * emb_ref[v : v + 1, :], axis=1, keepdims=True)
        xp[:, v : v + 1] = z
    raw = jnp.transpose(jnp.concatenate([xp[...]] * (128 // heads_half), axis=0))
    z = raw[0:8, 0:heads_half] + bias_ref[...]
    step = jnp.maximum(z, 0.0) + jnp.log1p(jnp.exp(-jnp.abs(z)))
    tab[tp, 32:36, 0:heads_half] = step[0:4]
    tab[tp, 36:37, 0:heads_half] = decay_ref[...]
    tab[tp, 37:38, 0:heads_half] = skip_ref[...]
    tab_copy = pltpu.make_async_remote_copy(
        src_ref=tab.at[tp], dst_ref=tab.at[tp], send_sem=tab_send, recv_sem=tab_recv,
        device_id={"tp": other}, device_id_type=MESH,
    )
    tab_copy.start()
    loads[4].wait()
    parts = project(wsbuf, 2 * state)
    for v in range(4):
        sproj[v : v + 1, :] = parts[v]
    wo_copy.start()

    for copy in id_copies:
        copy.wait()
    null = 4
    lane = lax.broadcasted_iota(jnp.int32, (8, block), 1)
    sub = lax.broadcasted_iota(jnp.int32, (8, block), 0)
    tri = (
        lax.broadcasted_iota(jnp.int32, (block, block), 0)
        <= lax.broadcasted_iota(jnp.int32, (block, block), 1)
    ).astype(BF)
    comp = [comp_ref[v] for v in range(4)]
    first_row = me * block + tp * rows
    running = jnp.zeros((8, 1), F32)
    before = jnp.zeros((8, 1), F32)
    through = jnp.zeros((8, 1), F32)
    for j in range(n):
        own = ids_all[j]
        blank = jnp.full((1, 128), null, jnp.int32)
        left = ids_all[j - 1][:, block - 128 :] if j > 0 else blank
        right = ids_all[j + 1][:, :128] if j < n - 1 else blank
        ext = rows_of(jnp.concatenate([left, own, right], axis=1), 8)
        cext = jnp.full_like(ext, null)
        for v in range(4):
            cext = jnp.where(ext == v, comp[v], cext)
        width = block + 256
        fwd = [pltpu.roll(ext, 3 - k, 1)[:, 128 : 128 + block] if k < 3 else ext[:, 128 : 128 + block] for k in range(4)]
        rev = [
            pltpu.roll(cext, width - (3 - k), 1)[:, 128 : 128 + block] if k < 3 else cext[:, 128 : 128 + block]
            for k in range(4)
        ]
        def pack(taps):
            return jnp.where(sub == 0, taps[0], jnp.where(sub == 1, taps[1], jnp.where(sub == 2, taps[2], taps[3])))
        def code(taps):
            return 64 * taps[0] + 16 * taps[1] + 4 * taps[2] + taps[3]
        code_f, code_r = code(fwd), code(rev)
        if j == 0:
            code_f = jnp.where(lane < 3, 256 + lane, code_f)
        if j == n - 1:
            code_r = jnp.where(lane >= block - 3, 264 - block + lane, code_r)
        taps_f[j] = jnp.where(sub == 4, code_f, pack(fwd))
        taps_r[j] = jnp.where(sub == 4, code_r, pack(rev))
        oh = (fwd[3] == sub).astype(F32)
        counts = dot(oh.astype(BF), tri) + running
        cnt_all[j] = counts
        oh_all[j] = oh
        running = running + jnp.sum(oh, axis=1, keepdims=True)
        t = lane + j * block
        before = before + jnp.sum(jnp.where(t < first_row, oh, 0.0), axis=1, keepdims=True)
        through = through + jnp.sum(jnp.where(t < first_row + rows, oh, 0.0), axis=1, keepdims=True)

    tab_copy.wait()
    lane1 = lax.broadcasted_iota(jnp.int32, (8, 128), 1)
    par = jnp.where(
        lane1 < heads_half, tab[0, 32:40, 0:128], pltpu.roll(tab[1, 32:40, 0:128], heads_half, 1)
    )
    par_t = jnp.transpose(jnp.concatenate([par] * 16, axis=0))[:heads]
    step_f = [par_t[:, v : v + 1] for v in range(4)]
    decay = par_t[:, 4:5] * LOG2E
    skb[...] = jnp.broadcast_to(par_t[:, 5:6], (heads, 128))
    step_r = []
    for v in range(4):
        s = jnp.zeros_like(step_f[0])
        for u in range(4):
            s = s + jnp.where(comp[v] == u, 1.0, 0.0) * step_f[u]
        step_r.append(s)
    log_f = [-decay * s for s in step_f]
    log_r = [-decay * s for s in step_r]

    def mixv(cols, r):
        acc = cols[0] * r[0:1]
        for v in range(1, 4):
            acc = acc + cols[v] * r[v : v + 1]
        return acc

    tlane = lax.broadcasted_iota(jnp.int32, (heads, block), 1)
    centry = lax.broadcasted_iota(jnp.int32, (384, block), 0)
    wf = jnp.zeros((2 * heads, 384), F32)
    wr = jnp.zeros((2 * heads, 384), F32)
    for j in range(n):
        counts, oh = cnt_all[j], oh_all[j]
        t = tlane + j * block
        ef = jnp.where(t < first_row, mixv(log_f, before - counts), 0.0)
        er = jnp.where(t >= first_row + rows, mixv(log_r, counts - oh - through), 0.0)
        pf = jnp.where(t < first_row, jnp.exp2(ef) * mixv(step_f, oh), 0.0)
        pr = jnp.where(t >= first_row + rows, jnp.exp2(er) * mixv(step_r, oh), 0.0)
        hot_f = (centry == taps_f[j, 4:5, :]).astype(BF)
        hot_r = (centry == taps_r[j, 4:5, :]).astype(BF)
        wf = wf + dot(jnp.concatenate(split2(pf), axis=0), hot_f, NT)
        wr = wr + dot(jnp.concatenate(split2(pr), axis=0), hot_r, NT)
    went[0] = wf[:heads] + wf[heads:]
    went[1] = wr[:heads] + wr[heads:]

    local_at = pl.ds(pl.multiple_of(tp * rows, 128), rows)
    counts = cnt_all[me, :, local_at]
    oh = oh_all[me, :, local_at]
    l_f = mixv(log_f, counts - before)
    l_r = mixv(log_r, through - counts + oh)
    lrow[0] = l_f
    lrow[1] = l_r
    lsrc[0] = l_f - jnp.log2(mixv(step_f, oh))
    lsrc[1] = l_r - jnp.log2(mixv(step_r, oh))

    def hot16(taps, width):
        r = lax.broadcasted_iota(jnp.int32, (16, width), 0)
        k, v = r // 4, r % 4
        chosen = jnp.where(k == 0, taps[0], jnp.where(k == 1, taps[1], jnp.where(k == 2, taps[2], taps[3])))
        hot = jnp.where(chosen == v, 1.0, 0.0)
        return jnp.concatenate([hot, hot, hot], axis=0).astype(BF)

    tf = taps_f[me, :, local_at]
    tr = taps_r[me, :, local_at]
    hot_rows = [hot16([x[k : k + 1] for k in range(4)], rows) for x in (tf, tr)]
    codes = lax.broadcasted_iota(jnp.int32, (8, 256), 1)
    edge_f = taps_f[0, :, 0:128]
    edge_r = pltpu.roll(taps_r[n - 1, :, block - 128 :], 8, 1)
    edge = jnp.where(lane1 < 4, edge_f, edge_r)
    table_taps = []
    for k in range(4):
        digit = (codes[0:1] // (4 ** (3 - k))) % 4
        table_taps.append(jnp.concatenate([digit, edge[k : k + 1]], axis=1))
    hot_table = hot16(table_taps, 384)

    def tap_table(conv, proj):
        width = conv.shape[1]
        r = lax.broadcasted_iota(jnp.int32, (16, width), 0)
        k, v = r // 4, r % 4
        c = jnp.where(k == 0, conv[0:1], jnp.where(k == 1, conv[1:2], jnp.where(k == 2, conv[2:3], conv[3:4])))
        p = jnp.where(v == 0, proj[0:1], jnp.where(v == 1, proj[1:2], jnp.where(v == 2, proj[2:3], proj[3:4])))
        return jnp.concatenate(split3(c * p), axis=0)

    ct_state = tap_table(cs_ref[...], sproj[0:4, :])
    btab[...] = silu(dot(ct_state[:, :state], hot_table, TN))
    ri = lax.broadcasted_iota(jnp.int32, (rows, rows), 0)
    ci = lax.broadcasted_iota(jnp.int32, (rows, rows), 1)
    for s in range(2):
        maps = silu(dot(hot_rows[s], ct_state, TN))
        cmat[s] = maps[:, state:]
        seen = (ri >= ci) if s == 0 else (ri <= ci)
        gmat[s] = jnp.where(seen, dot3(maps[:, state:], maps[:, :state], NT), 0.0)

    own_hot = jnp.concatenate([oh[0:8]] * 3 + [jnp.zeros((24, rows), F32)], axis=0).astype(BF)
    rev_oh = jnp.zeros((8, rows), F32)
    sub_r = lax.broadcasted_iota(jnp.int32, (8, rows), 0)
    rev_oh = (tr[3:4] == sub_r).astype(F32)
    rev_hot = jnp.concatenate([rev_oh] * 3 + [jnp.zeros((24, rows), F32)], axis=0).astype(BF)
    for p in range(2):
        for q in range(4):
            width = half // 4
            lo = q * width
            at = slice(p * half + lo, p * half + lo + width)
            ct = tap_table(tab[p, 16:20, lo : lo + width], tab[p, 8:12, lo : lo + width])
            vtab[0:256, at] = silu(dot(hot_table[:, :256], ct, TN))
            vtab[256:272, at] = silu(dot(hot_table[:, 256:], ct, TN)[:16])
            g8 = silu(tab[p, 0:8, lo : lo + width])
            r8 = lax.broadcasted_iota(jnp.int32, (8, width), 0)
            g8 = jnp.where(r8 < 4, g8, 0.0)
            gh, gm, gl = split3(g8)
            gt = jnp.concatenate(
                [gh.astype(F32), gm.astype(F32), gl.astype(F32), jnp.zeros((24, width), F32)], axis=0
            ).astype(BF)
            for s in range(2):
                xs[s, :, at] = silu(dot(hot_rows[s], ct, TN))
                gate[s, :, at] = dot((own_hot, rev_hot)[s], gt, TN)

    accs[...] = jnp.zeros_like(accs)
    mid = rows // 2
    low = lax.broadcasted_iota(jnp.int32, (rows, 128), 1) < 64
    tri_r = lax.broadcasted_iota(jnp.int32, (mid, mid), 0)
    tri_c = lax.broadcasted_iota(jnp.int32, (mid, mid), 1)
    for s in range(2):
        ccat[s] = jnp.concatenate(split2(cmat[s]), axis=1)
    b_hi, b_lo = split2(btab[...])
    bcat[...] = jnp.concatenate([b_hi[:, :256], b_lo[:, :256]], axis=0)
    e_hi = b_hi[:, 256:].astype(F32)
    e_lo = pltpu.roll(b_lo[:, 256:].astype(F32), 16, 1)
    elane = lax.broadcasted_iota(jnp.int32, (state, 128), 1)
    becat[...] = jnp.where(elane < 16, e_hi, jnp.where(elane < 32, e_lo, 0.0)).astype(BF)

    def heads_rows(ref, s, h, at):
        return jnp.concatenate(
            [rows_of(ref[s, pl.ds(h, 1), :][:, at], 64), rows_of(ref[s, pl.ds(h + 1, 1), :][:, at], 64)], axis=0
        )

    def pair(q, carry):
        at = pl.ds(pl.multiple_of(q * 128, 128), 128)
        vt, ve = vtab[0:256, at], vtab[256:272, at]
        sk = jnp.where(low[0:1], skb[pl.ds(2 * q, 1), :], skb[pl.ds(2 * q + 1, 1), :])
        for s in range(2):
            near = slice(0, mid) if s == 0 else slice(mid, rows)
            far = slice(mid, rows) if s == 0 else slice(0, mid)
            seen = (tri_r >= tri_c) if s == 0 else (tri_r <= tri_c)
            x = xs[s, :, at]
            x_hi, x_lo = split2(x)
            both = jnp.concatenate([x_hi, x_lo], axis=1)
            near_both = jnp.concatenate([both[near], both[near]], axis=0)
            near_l, far_hi, far_lo, cols = [], [], [], []
            for a in range(2):
                h = 2 * q + a
                col = jnp.transpose(rows_of(lrow[s, pl.ds(h, 1), :], 128))
                src = lsrc[s, pl.ds(h, 1), :]
                def decayed(i, j, masked):
                    e = col[i] - src[:, j]
                    if masked:
                        e = jnp.where(seen, e, -1e30)
                    return split2(jnp.exp2(e) * gmat[s, i, j])
                nn_hi, nn_lo = decayed(near, near, True)
                ff_hi, ff_lo = decayed(far, far, True)
                fn_hi, fn_lo = decayed(far, near, False)
                near_l.append(jnp.concatenate([nn_hi, nn_lo], axis=1))
                order = (fn_hi, ff_hi) if s == 0 else (ff_hi, fn_hi)
                far_hi.append(jnp.concatenate(order, axis=1))
                order = (fn_lo, ff_lo) if s == 0 else (ff_lo, fn_lo)
                far_lo.append(jnp.concatenate(order, axis=1))
                cols.append(col)
            rn = dot(jnp.concatenate(near_l, axis=0), near_both)
            rf = dot(jnp.concatenate(far_hi, axis=0), both)
            rl = dot(jnp.concatenate(far_lo, axis=0), x_hi)
            rn = rn[:, :128] + rn[:, 128:]
            rf = rf[:, :128] + rf[:, 128:] + rl
            lowm = low[:mid]
            yn = jnp.where(lowm, rn[:mid], rn[mid:])
            yf = jnp.where(lowm, rf[:mid], rf[mid:])
            y = jnp.concatenate([yn, yf] if s == 0 else [yf, yn], axis=0)
            w = jnp.transpose(heads_rows(went, s, 2 * q, slice(0, 256)))
            we = jnp.transpose(heads_rows(went, s, 2 * q, slice(256, 384)))[:16]
            vw = jnp.concatenate(split2(vt * w), axis=1)
            vwe = jnp.concatenate(split2(ve * we), axis=1)
            vwe = jnp.concatenate([vwe, vwe], axis=0)
            r = dot(bcat[...], vw)
            r = r[:state] + r[state:] + dot(becat[:, 0:32], vwe)
            mem = r[:, :128] + r[:, 128:]
            m2 = jnp.concatenate(split2(mem), axis=1)
            carried = dot(ccat[s], jnp.concatenate([m2, m2], axis=0))
            carried = carried[:, :128] + carried[:, 128:]
            y = y + carried * jnp.exp2(jnp.where(low, cols[0], cols[1]))
            g = (y + sk * x) * gate[s, :, at]
            gated[s, :, at] = g
            accs[s] = accs[s] + g * g
        return carry

    lax.fori_loop(0, pairs, pair, 0, unroll=2)

    scales = [
        lax.rsqrt(jnp.sum(accs[s], axis=1, keepdims=True) / inner + EPSILON) for s in range(2)
    ]
    wo_copy.wait()
    wo_remote.wait()
    out_ref[...] = jnp.zeros_like(out_ref)
    step_k = 256
    for p in range(2):
        def project_out(q, carry):
            lo = pl.multiple_of(q * step_k, step_k)
            at = pl.ds(pl.multiple_of(p * half + q * step_k, step_k), step_k)
            mixed = (gated[0, :, at] * scales[0] + gated[1, :, at] * scales[1]) * tab[
                p, 24:25, pl.ds(lo, step_k)
            ]
            out_ref[...] += dot3(mixed, wout[p, pl.ds(lo, step_k), :])
            return carry

        lax.fori_loop(0, half // step_k, project_out, 0)


def local(
    nucleotides, complement, embedding, w_gate, w_value, w_state, w_step, step_bias,
    decay_rate, conv_value, conv_state, skip_gain, norm_weight, w_out,
):
    n = lax.axis_size("ctx")
    block = nucleotides.shape[0]
    rows = block // 2
    half = w_gate.shape[1]
    depth = w_gate.shape[0]
    inner = 2 * half
    heads = 2 * step_bias.shape[0]
    state = w_state.shape[1] // 2
    vm = pl.BlockSpec(memory_space=pltpu.VMEM)
    hbm = pl.BlockSpec(memory_space=pl.ANY)
    sm = pl.BlockSpec(memory_space=pltpu.SMEM)
    dma = pltpu.SemaphoreType.DMA
    return pl.pallas_call(
        functools.partial(kernel, n),
        out_shape=jax.ShapeDtypeStruct((rows, w_out.shape[1]), F32),
        in_specs=[vm, sm, vm, hbm, hbm, hbm, vm, vm, vm, vm, vm, vm, vm, hbm],
        out_specs=vm,
        scratch_shapes=[
            pltpu.VMEM((n, 1, block), jnp.int32),
            pltpu.VMEM((2, 40, half), F32),
            pltpu.VMEM((2, half, w_out.shape[1]), F32),
            pltpu.VMEM((4, depth, half // 2), F32),
            pltpu.VMEM((depth, 2 * state), F32),
            pltpu.VMEM((4, depth, 128), F32),
            pltpu.VMEM((8, 2 * state), F32),
            pltpu.VMEM((n, 8, block), jnp.int32),
            pltpu.VMEM((n, 8, block), jnp.int32),
            pltpu.VMEM((n, 8, block), F32),
            pltpu.VMEM((n, 8, block), F32),
            pltpu.VMEM((272, inner), F32),
            pltpu.VMEM((2, rows, inner), F32),
            pltpu.VMEM((heads // 2, 128), F32),
            pltpu.VMEM((2, rows, inner), F32),
            pltpu.VMEM((2, rows, inner), F32),
            pltpu.VMEM((2, heads, rows), F32),
            pltpu.VMEM((2, heads, rows), F32),
            pltpu.VMEM((2, heads, 384), F32),
            pltpu.VMEM((heads, 128), F32),
            pltpu.VMEM((2, rows, rows), F32),
            pltpu.VMEM((2, rows, state), F32),
            pltpu.VMEM((state, 384), F32),
            pltpu.VMEM((2, rows, 128), F32),
            pltpu.VMEM((2, rows, 2 * state), BF),
            pltpu.VMEM((2 * state, 256), BF),
            pltpu.VMEM((state, 128), BF),
            dma((5,)),
            dma((n - 1,)),
            dma((n - 1,)),
            dma, dma, dma, dma, dma,
        ],
        compiler_params=pltpu.CompilerParams(
            collective_id=0, has_side_effects=True, vmem_limit_bytes=60 * 1024 * 1024
        ),
    )(
        nucleotides[None, :], complement, embedding, w_gate, w_value, w_state, w_step.T,
        step_bias[None, :], decay_rate[None, :], conv_value, conv_state, skip_gain[None, :],
        norm_weight[None, :], w_out,
    )


def solution(mesh):
    placed = (
        P(("dp", "ctx")), P(), P(), P(None, "tp"), P(None, "tp"), P(), P(None, "tp"),
        P("tp"), P("tp"), P(None, "tp"), P(), P("tp"), P("tp"), P("tp", None),
    )
    return jax.shard_map(
        local, mesh=mesh, in_specs=placed, out_specs=P(("dp", "ctx", "tp"), None), check_vma=False
    )
```
